256 devices in a mesh: pos: 32 (over x, z), grp: 8 (over y, core).
Axes of the slice: x: 4, y: 4, z: 8, core: 2. Of those that a mesh axis runs over, the one named last changes fastest.
Arguments:
- key_cache: bfloat16 [262144, 2048], P(('grp', 'pos')), parts along dimension 0, may hold values from -60 to 60
- init_basis: float32 [16384, 256], P('grp'), parts along dimension 0, may hold values from -0.125 to 0.125
Outputs:
- basis_scaled: float32 [16384, 256], P('grp'), parts along dimension 0
- latents: bfloat16 [262144, 256], P(('grp', 'pos')), parts along dimension 0
The draws below stay inside these ranges and needn't reach their ends.
There are 8 independent parts, one for each index of `grp`. The reference program is written for one: setup_inputs(seed, part) draws one part's arguments, and reference() takes and returns one part's arrays. A program takes and returns all parts, laid end to end along the dimension named above; each array names one. Nothing has to cross between parts.
All inputs are finite; a program needn't handle non-finite values.
Results may differ from the reference program's by a relative error of at most 0.0095.
Values may be sent and summed in bfloat16 or wider, within the bound.
No kernel may reach another device: no remote copies, remote signals or barrier semaphores. Data moves between devices by JAX's collectives and lax.ppermute only.
A program may use at most 64 MiB of HBM per device.

```python
import jax
import jax.numpy as jnp
from jax import lax

W = 2048
R = 256
ITERS = 3
TOK_DEV = 1024
TOKENS = 32768
N_POS = 32


def draw_key_cache(key, part):
    key = jax.random.fold_in(key, 11)
    first = jax.random.fold_in(key, 0)
    second = jax.random.fold_in(key, 1)
    third = jax.random.fold_in(key, 2)
    fifth = jax.random.fold_in(key, 4)
    base = jnp.clip(jax.random.normal(first, (TOKENS, W), jnp.float32), -4.0, 4.0)
    row_scale = jnp.exp(jax.random.uniform(second, (TOKENS, 1), jnp.float32, jnp.log(0.5), jnp.log(5.0)))
    ramp = jnp.sqrt(1.0 + 2.0 * jnp.arange(TOKENS, dtype=jnp.float32) / TOKENS).reshape(TOKENS, 1)
    column_scale = jnp.exp(jax.random.uniform(third, (1, W), jnp.float32, jnp.log(0.5), jnp.log(2.0)))
    block_count = TOKENS // TOK_DEV
    block_scale = jnp.exp(jax.random.uniform(fifth, (block_count, 1, W), jnp.float32, jnp.log(0.3), jnp.log(3.0)))
    values = base * row_scale * ramp * column_scale
    values = (values.reshape(block_count, TOK_DEV, W) * block_scale).reshape(TOKENS, W)
    values = jnp.clip(values, -60.0, 60.0)
    return values.astype(jnp.bfloat16)


def centred(stream_key, dims, spread, most, held_as=jnp.bfloat16):
    return jnp.clip(spread * jax.random.normal(stream_key, dims, jnp.float32), -most, most).astype(held_as)


def setup_inputs(seed: int = 0, part: int = 0) -> dict:
    splits = jax.random.split(jax.random.key(seed), 3)
    own_keys = jax.random.split(jax.random.fold_in(splits[2], part), 3)
    key_cache = draw_key_cache(jax.random.fold_in(jax.random.fold_in(splits[2], part), 71), part)
    init_basis = centred(own_keys[1], (W, R), W ** -0.5, 0.125, jnp.float32)
    return {"key_cache": key_cache, "init_basis": init_basis}


def orthonormal(summed):
    gram_matrix = jnp.dot(summed.T, summed, precision=lax.Precision.HIGHEST)
    factor = jnp.linalg.cholesky(gram_matrix)
    return jax.scipy.linalg.solve_triangular(factor, summed.T, lower=True).T

def reference(key_cache, init_basis):
    basis = init_basis
    for sweep in range(ITERS):
        rounded = basis.astype(jnp.bfloat16)
        projected = jnp.dot(key_cache.astype(jnp.float32), rounded.astype(jnp.float32), preferred_element_type=jnp.float32).astype(jnp.bfloat16)
        summed = lax.dot_general(key_cache.astype(jnp.float32), projected.astype(jnp.float32), (((0,), (0,)), ((), ())), preferred_element_type=jnp.float32)
        basis = orthonormal(summed)
    compressed = jnp.dot(key_cache.astype(jnp.float32), basis.astype(jnp.bfloat16).astype(jnp.float32), preferred_element_type=jnp.float32).astype(jnp.bfloat16)
    blocks = compressed.reshape(N_POS, N_POS, TOK_DEV // N_POS, R)
    latents = jnp.transpose(blocks, (1, 0, 2, 3)).reshape(TOKENS, R)
    return (jnp.sqrt(jnp.float32(W)) * basis, latents)
```

```python
import functools

import jax
import jax.numpy as jnp
from jax import lax
from jax.experimental import pallas as pl
from jax.experimental.pallas import tpu as pltpu
from jax.sharding import Mesh
from jax.sharding import PartitionSpec as P

ITERS = 3
NX = 4
NZ = 8
NB = 32
VMEM_BYTES = 40 * 1024 * 1024
F32 = jnp.float32
BF16 = jnp.bfloat16

NN = (((1,), (0,)), ((), ()))
NT = (((1,), (1,)), ((), ()))
TN = (((0,), (0,)), ((), ()))


def dot(a, b, dims):
    return lax.dot_general(a, b, dims, preferred_element_type=F32)


def exact_dot(a, b, dims):
    return lax.dot_general(a, b, dims, precision=lax.Precision.HIGHEST, preferred_element_type=F32)


def eliminate(rows, inverse, block):
    n = rows.shape[1]
    row_id = lax.broadcasted_iota(jnp.int32, (NB, 1), 0)
    pivots = jnp.ones((NB, 1), F32)
    for strip in range(NB // 8):
        first = block * NB + strip * 8
        columns = [rows[:, first + s : first + s + 1] for s in range(8)]
        columns = [jnp.broadcast_to(c, (NB, 128)) for c in columns]
        for s in range(8):
            k = strip * 8 + s
            pivot = columns[s][k : k + 1, :]
            below = jnp.where(row_id > k, columns[s] * (1.0 / pivot), 0.0)
            pivots = jnp.where(row_id == k, pivot, pivots)
            for later in range(s + 1, 8):
                columns[later] = columns[later] - below * columns[later][k : k + 1, :]
            wide = jnp.concatenate([below] * (n // 128), axis=1)
            rows = rows - wide * rows[k : k + 1, :]
            inverse = inverse - wide * inverse[k : k + 1, :]
    scale = lax.rsqrt(pivots)
    scale = jnp.concatenate([scale] * (n // 128), axis=1)
    return rows * scale, inverse * scale


def inverse_factor(gram, inv):
    n = gram.shape[0]
    eye = lax.broadcasted_iota(jnp.int32, (n, n), 0) == lax.broadcasted_iota(jnp.int32, (n, n), 1)
    inv[...] = eye.astype(F32)
    for block in range(n // NB):
        here = pl.ds(block * NB, NB)
        upper, lower = eliminate(gram[here, :], inv[here, :], block)
        inv[here, :] = lower
        done = (block + 1) * NB
        if done < n:
            factor = upper.T[done:, :]
            rest = pl.ds(done, n - done)
            gram[rest, :] = gram[rest, :] - exact_dot(factor, upper, NN)
            inv[rest, :] = inv[rest, :] - exact_dot(factor, lower, NN)


def split(a):
    high = a.astype(BF16)
    rest = a - high.astype(F32)
    mid = rest.astype(BF16)
    low = (rest - mid.astype(F32)).astype(BF16)
    return high, mid, low


def products(keys, basis, out):
    width = basis[0].shape[1]
    projected = 0.0
    for x in range(NX):
        projected = projected + dot(basis[x], keys[:, x * width : (x + 1) * width], NT)
    projected = projected.astype(BF16)
    for x in range(NX):
        out[x] = dot(projected, keys[:, x * width : (x + 1) * width], NN).astype(BF16)


def first_kernel(keys, basis, out):
    products(keys, [basis[x] for x in range(NX)], out)


def factor_of(summed, gram, inv):
    total = 0.0
    for x in range(NX):
        total = total + dot(summed[x], summed[x], NT)
    gram[...] = total
    inverse_factor(gram, inv)
    return split(inv[...])


def middle_kernel(summed, keys_hbm, out, gram, inv, keys, sem):
    copy = pltpu.make_async_copy(keys_hbm, keys, sem)
    copy.start()
    parts = factor_of(summed, gram, inv)
    basis = [sum(dot(p, summed[x], NN) for p in parts).astype(BF16) for x in range(NX)]
    copy.wait()
    products(keys, basis, out)


def last_kernel(summed, keys_hbm, basis_out, out, gram, inv, keys, sem):
    copy = pltpu.make_async_copy(keys_hbm, keys, sem)
    copy.start()
    parts = factor_of(summed, gram, inv)
    width = summed.shape[2]
    scale = jnp.sqrt(F32(NX * width))
    basis = [sum(dot(p, summed[x], NN) for p in parts) for x in range(NX)]
    for x in range(NX):
        basis_out[pl.ds(x * width, width), :] = (basis[x] * scale).T
    copy.wait()
    compressed = 0.0
    for x in range(NX):
        compressed = compressed + dot(keys[:, x * width : (x + 1) * width], basis[x].astype(BF16), NT)
    out[...] = compressed.astype(BF16)


def call(body, out_shape, operands, in_hbm, scratch):
    spec = [pl.BlockSpec(memory_space=pl.ANY if h else pltpu.VMEM) for h in in_hbm]
    return pl.pallas_call(
        body,
        out_shape=out_shape,
        in_specs=spec,
        out_specs=jax.tree.map(lambda _: pl.BlockSpec(memory_space=pltpu.VMEM), out_shape),
        scratch_shapes=scratch,
        compiler_params=pltpu.CompilerParams(vmem_limit_bytes=VMEM_BYTES),
    )(*operands)


def sum_and_spread(local_term):
    _, rank, width = local_term.shape
    part = rank // NZ
    terms = lax.all_to_all(local_term, "x", 0, 0, tiled=True)
    total = jnp.sum(terms.astype(F32), axis=0).astype(BF16).reshape(NZ, part, width)
    terms = lax.all_to_all(total, "z", 0, 0, tiled=True)
    total = jnp.sum(terms.astype(F32), axis=0).astype(BF16)
    total = jnp.broadcast_to(total[None], (NZ, part, width))
    block = lax.all_to_all(total, "z", 0, 0, tiled=True).reshape(1, rank, width)
    return lax.all_to_all(jnp.broadcast_to(block, (NX, rank, width)), "x", 0, 0, tiled=True)


def local(key_cache, init_basis):
    positions, features = key_cache.shape
    rank = init_basis.shape[1]
    width = features // NX
    shape = jax.ShapeDtypeStruct
    scratch = [
        pltpu.VMEM((rank, rank), F32),
        pltpu.VMEM((rank, rank), F32),
        pltpu.VMEM((positions, features), BF16),
        pltpu.SemaphoreType.DMA,
    ]
    blocks = shape((NX, rank, width), BF16)
    rounded = init_basis.astype(BF16).reshape(NX, width, rank).transpose(0, 2, 1)
    term = call(first_kernel, blocks, (key_cache, rounded), (False, False), [])
    for sweep in range(ITERS - 1):
        summed = sum_and_spread(term)
        term = call(middle_kernel, blocks, (summed, key_cache), (False, True), scratch)
    summed = sum_and_spread(term)
    outs = (shape((features, rank), F32), shape((positions, rank), BF16))
    basis, compressed = call(last_kernel, outs, (summed, key_cache), (False, True), scratch)
    latents = lax.all_to_all(compressed, ("x", "z"), split_axis=0, concat_axis=0, tiled=True)
    return basis, latents


def solution(mesh):
    grid = Mesh(mesh.devices.reshape(NX, NZ, -1), ("x", "z", "grp"))
    return jax.shard_map(
        local,
        mesh=grid,
        in_specs=(P(("grp", "x", "z"), None), P("grp", None)),
        out_specs=(P("grp", None), P(("grp", "x", "z"), None)),
        check_vma=False,
    )
```

```python
import functools

import jax
import jax.numpy as jnp
from jax import lax
from jax.experimental import pallas as pl
from jax.experimental.pallas import tpu as pltpu
from jax.sharding import Mesh
from jax.sharding import PartitionSpec as P

ITERS = 3
NX = 4
NZ_HIGH = 4
NZ_LOW = 2
NB = 32
AXES = ("x", "z_high", "z_low", "grp")
VMEM_BYTES = 40 * 1024 * 1024
F32 = jnp.float32
BF16 = jnp.bfloat16

NN = (((1,), (0,)), ((), ()))
NT = (((1,), (1,)), ((), ()))
TN = (((0,), (0,)), ((), ()))


def dot(a, b, dims):
    return lax.dot_general(a, b, dims, preferred_element_type=F32)


def exact_dot(a, b, dims):
    return lax.dot_general(a, b, dims, precision=lax.Precision.HIGHEST, preferred_element_type=F32)


def eliminate(rows, inverse, block):
    n = rows.shape[1]
    row_id = lax.broadcasted_iota(jnp.int32, (NB, 1), 0)
    pivots = jnp.ones((NB, 1), F32)
    for strip in range(NB // 8):
        first = block * NB + strip * 8
        columns = [rows[:, first + s : first + s + 1] for s in range(8)]
        columns = [jnp.broadcast_to(c, (NB, 128)) for c in columns]
        for s in range(8):
            k = strip * 8 + s
            pivot = columns[s][k : k + 1, :]
            below = jnp.where(row_id > k, columns[s] * (1.0 / pivot), 0.0)
            pivots = jnp.where(row_id == k, pivot, pivots)
            for later in range(s + 1, 8):
                columns[later] = columns[later] - below * columns[later][k : k + 1, :]
            wide = jnp.concatenate([below] * (n // 128), axis=1)
            rows = rows - wide * rows[k : k + 1, :]
            inverse = inverse - wide * inverse[k : k + 1, :]
    scale = lax.rsqrt(pivots)
    scale = jnp.concatenate([scale] * (n // 128), axis=1)
    return rows * scale, inverse * scale


def inverse_factor(gram, inv):
    n = gram.shape[0]
    eye = lax.broadcasted_iota(jnp.int32, (n, n), 0) == lax.broadcasted_iota(jnp.int32, (n, n), 1)
    inv[...] = eye.astype(F32)
    for block in range(n // NB):
        here = pl.ds(block * NB, NB)
        upper, lower = eliminate(gram[here, :], inv[here, :], block)
        inv[here, :] = lower
        done = (block + 1) * NB
        if done < n:
            factor = upper.T[done:, :]
            rest = pl.ds(done, n - done)
            gram[rest, :] = gram[rest, :] - exact_dot(factor, upper, NN)
            inv[rest, :] = inv[rest, :] - exact_dot(factor, lower, NN)


def split(a):
    high = a.astype(BF16)
    rest = a - high.astype(F32)
    mid = rest.astype(BF16)
    low = (rest - mid.astype(F32)).astype(BF16)
    return high, mid, low


def products(keys, basis, out):
    width = basis[0].shape[1]
    projected = 0.0
    for x in range(NX):
        projected = projected + dot(basis[x], keys[:, x * width : (x + 1) * width], NT)
    projected = projected.astype(BF16)
    for x in range(NX):
        out[x] = dot(projected, keys[:, x * width : (x + 1) * width], NN).astype(BF16)


def first_kernel(keys, basis, out):
    products(keys, [basis[x] for x in range(NX)], out)


def factor_of(summed, gram, inv):
    total = 0.0
    for x in range(NX):
        total = total + dot(summed[x], summed[x], NT)
    gram[...] = total
    inverse_factor(gram, inv)
    return split(inv[...])


def middle_kernel(summed, keys_hbm, out, gram, inv, keys, sem):
    copy = pltpu.make_async_copy(keys_hbm, keys, sem)
    copy.start()
    parts = factor_of(summed, gram, inv)
    basis = [sum(dot(p, summed[x], NN) for p in parts).astype(BF16) for x in range(NX)]
    copy.wait()
    products(keys, basis, out)


def last_kernel(summed, keys_hbm, basis_out, out, gram, inv, keys, sem):
    copy = pltpu.make_async_copy(keys_hbm, keys, sem)
    copy.start()
    parts = factor_of(summed, gram, inv)
    width = summed.shape[2]
    scale = jnp.sqrt(F32(NX * width))
    basis = [sum(dot(p, summed[x], NN) for p in parts) for x in range(NX)]
    for x in range(NX):
        basis_out[pl.ds(x * width, width), :] = (basis[x] * scale).T
    copy.wait()
    compressed = 0.0
    for x in range(NX):
        compressed = compressed + dot(keys[:, x * width : (x + 1) * width], basis[x].astype(BF16), NT)
    out[...] = compressed.astype(BF16)


def call(body, out_shape, operands, in_hbm, scratch):
    spec = [pl.BlockSpec(memory_space=pl.ANY if h else pltpu.VMEM) for h in in_hbm]
    return pl.pallas_call(
        body,
        out_shape=out_shape,
        in_specs=spec,
        out_specs=jax.tree.map(lambda _: pl.BlockSpec(memory_space=pltpu.VMEM), out_shape),
        scratch_shapes=scratch,
        compiler_params=pltpu.CompilerParams(vmem_limit_bytes=VMEM_BYTES),
    )(*operands)


def sum_and_spread(local_term):
    _, rank, width = local_term.shape
    near = NX * NZ_LOW
    part = rank // NZ_LOW
    terms = local_term.reshape(near, part, width)
    terms = lax.all_to_all(terms, ("x", "z_low"), 0, 0, tiled=True)
    own = jnp.sum(terms.astype(F32), axis=0).astype(BF16)
    first, second, third = (
        lax.ppermute(own, "z_high", [(i, (i + step) % NZ_HIGH) for i in range(NZ_HIGH)]).astype(F32)
        for step in range(1, NZ_HIGH)
    )
    total = ((own.astype(F32) + second) + (first + third)).astype(BF16)
    total = jnp.broadcast_to(total[None], (near, part, width))
    blocks = lax.all_to_all(total, ("x", "z_low"), 0, 0, tiled=True)
    return blocks.reshape(NX, rank, width)


def local(key_cache, init_basis):
    positions, features = key_cache.shape
    rank = init_basis.shape[1]
    width = features // NX
    shape = jax.ShapeDtypeStruct
    scratch = [
        pltpu.VMEM((rank, rank), F32),
        pltpu.VMEM((rank, rank), F32),
        pltpu.VMEM((positions, features), BF16),
        pltpu.SemaphoreType.DMA,
    ]
    blocks = shape((NX, rank, width), BF16)
    rounded = init_basis.astype(BF16).reshape(NX, width, rank).transpose(0, 2, 1)
    term = call(first_kernel, blocks, (key_cache, rounded), (False, False), [])
    for sweep in range(ITERS - 1):
        summed = sum_and_spread(term)
        term = call(middle_kernel, blocks, (summed, key_cache), (False, True), scratch)
    summed = sum_and_spread(term)
    outs = (shape((features, rank), F32), shape((positions, rank), BF16))
    basis, compressed = call(last_kernel, outs, (summed, key_cache), (False, True), scratch)
    latents = lax.all_to_all(compressed, ("x", "z_high", "z_low"), split_axis=0, concat_axis=0, tiled=True)
    return basis, latents


def solution(mesh):
    grid = Mesh(mesh.devices.reshape(NX, NZ_HIGH, NZ_LOW, -1), AXES)
    return jax.shard_map(
        local,
        mesh=grid,
        in_specs=(P(("grp",) + AXES[:3], None), P("grp", None)),
        out_specs=(P("grp", None), P(("grp",) + AXES[:3], None)),
        check_vma=False,
    )
```

```python
import jax
import jax.numpy as jnp
from jax import lax
from jax.experimental import pallas as pl
from jax.experimental.pallas import tpu as pltpu
from jax.sharding import Mesh
from jax.sharding import PartitionSpec as P

ITERS = 3
NX = 4
NZ_HIGH = 4
NZ_LOW = 2
NB = 32
GROUP = 8
STRIP = 16
AXES = ("x", "z_high", "z_low", "grp")
VMEM_BYTES = 59_500_000
F32 = jnp.float32
BF16 = jnp.bfloat16

NN = (((1,), (0,)), ((), ()))
NT = (((1,), (1,)), ((), ()))
TN = (((0,), (0,)), ((), ()))


def dot(a, b, dims):
    return lax.dot_general(a, b, dims, preferred_element_type=F32)


def split(a):
    high = a.astype(BF16)
    rest = a - high.astype(F32)
    mid = rest.astype(BF16)
    low = (rest - mid.astype(F32)).astype(BF16)
    return high, mid, low


def stacked(parts, order):
    return jnp.concatenate([parts[i] for i in order], axis=0)


LEFT = (0, 0, 1, 0, 2, 1)
RIGHT = (0, 1, 0, 2, 0, 1)


def widen(a, lanes):
    return jnp.concatenate([a] * (lanes // 128), axis=1) if lanes > 128 else a


def eliminate(rows, inverse, column):
    row_id = lax.broadcasted_iota(jnp.int32, (GROUP, 128), 0)
    groups = len(rows)
    rows, inverse = list(rows), list(inverse)
    lanes, inverse_lanes = rows[0].shape[1], inverse[0].shape[1]
    for first in range(0, groups, STRIP // GROUP):
        held = {}
        for g in range(first, groups):
            at = column + first * GROUP
            held[g] = [
                jnp.broadcast_to(rows[g][:, at + s : at + s + 1], (GROUP, 128)) for s in range(STRIP)
            ]
        for s in range(STRIP):
            own, k = first + s // GROUP, s % GROUP
            if k == 0:
                pivots = jnp.ones((GROUP, 128), F32)
            pivot = held[own][s][k : k + 1, :]
            reciprocal = 1.0 / pivot
            pivots = jnp.where(row_id == k, pivot, pivots)
            heads = [held[own][t][k : k + 1, :] * reciprocal for t in range(s + 1, STRIP)]
            pivot_row, pivot_inverse = rows[own][k : k + 1, :], inverse[own][k : k + 1, :]
            for g in range(own, groups):
                base = held[g][s]
                for t in range(s + 1, STRIP):
                    held[g][t] = held[g][t] - base * heads[t - s - 1]
                factor = base * reciprocal
                if g == own:
                    factor = jnp.where(row_id > k, factor, 0.0)
                rows[g] = rows[g] - widen(factor, lanes) * pivot_row
                inverse[g] = inverse[g] - widen(factor, inverse_lanes) * pivot_inverse
            if k == GROUP - 1:
                scale = lax.rsqrt(pivots)
                rows[own] = rows[own] * widen(scale, lanes)
                inverse[own] = inverse[own] * widen(scale, inverse_lanes)
    return rows, inverse


def inverse_factor(gram, inv):
    n = gram.shape[0]
    eye = lax.broadcasted_iota(jnp.int32, (n, n), 0) == lax.broadcasted_iota(jnp.int32, (n, n), 1)
    inv[...] = eye.astype(F32)
    for start in range(0, n, NB):
        done = start + NB
        left = start // 128 * 128
        right = -(-done // 128) * 128
        groups = [pl.ds(start + g, GROUP) for g in range(0, NB, GROUP)]
        upper, lower = eliminate(
            [gram[g, left:] for g in groups], [inv[g, :right] for g in groups], start - left
        )
        upper, lower = jnp.concatenate(upper, axis=0), jnp.concatenate(lower, axis=0)
        inv[pl.ds(start, NB), :right] = lower
        if done < n:
            keep = done // 128 * 128
            upper_parts = split(upper[:, keep - left :])
            factor = stacked(upper_parts, LEFT)
            rest = pl.ds(done, n - done)
            update = dot(factor, stacked(upper_parts, RIGHT), TN)
            gram[rest, keep:] = gram[rest, keep:] - update[done - keep :]
            update = dot(factor, stacked(split(lower), RIGHT), TN)
            inv[rest, :right] = inv[rest, :right] - update[done - keep :]


def products(keys, basis, out):
    width = basis[0].shape[1]
    projected = 0.0
    for x in range(NX):
        projected = projected + dot(basis[x], keys[:, x * width : (x + 1) * width], NT)
    projected = projected.astype(BF16)
    for x in range(NX):
        out[x] = dot(projected, keys[:, x * width : (x + 1) * width], NN).astype(BF16)


def first_kernel(keys_hbm, basis_hbm, out, keys, basis, key_sems, basis_sems):
    width = keys.shape[1] // NX
    copies = []
    for x in range(NX):
        part = pl.ds(x * width, width)
        of_basis = pltpu.make_async_copy(basis_hbm.at[part, :], basis.at[part, :], basis_sems.at[x])
        of_keys = pltpu.make_async_copy(keys_hbm.at[:, part], keys.at[:, part], key_sems.at[x])
        of_basis.start()
        of_keys.start()
        copies.append((of_basis, of_keys))
    projected = 0.0
    for x, (of_basis, of_keys) in enumerate(copies):
        of_basis.wait()
        rounded = basis[pl.ds(x * width, width), :].T.astype(BF16)
        of_keys.wait()
        projected = projected + dot(rounded, keys[:, x * width : (x + 1) * width], NT)
    projected = projected.astype(BF16)
    for x in range(NX):
        out[x] = dot(projected, keys[:, x * width : (x + 1) * width], NN).astype(BF16)


def basis_blocks(summed, inv):
    high, mid, _ = split(inv)
    return [dot(high, summed[x], NN) + dot(mid, summed[x], NN) for x in range(NX)]


def factorize(summed, gram, inv):
    total = 0.0
    for x in range(NX):
        total = total + dot(summed[x], summed[x], NT)
    gram[...] = total
    inverse_factor(gram, inv)


def middle_kernel(summed, keys_hbm, out, gram, inv, keys, sem):
    copy = pltpu.make_async_copy(keys_hbm, keys, sem)
    copy.start()
    factorize(summed, gram, inv)
    basis = [b.astype(BF16) for b in basis_blocks(summed, inv[...])]
    copy.wait()
    products(keys, basis, out)


def last_kernel(summed, keys_hbm, inv, out, gram, keys, sem):
    copy = pltpu.make_async_copy(keys_hbm, keys, sem)
    copy.start()
    factorize(summed, gram, inv)
    width = summed.shape[2]
    basis = [b.astype(BF16) for b in basis_blocks(summed, inv[...])]
    copy.wait()
    compressed = 0.0
    for x in range(NX):
        compressed = compressed + dot(keys[:, x * width : (x + 1) * width], basis[x], NT)
    out[...] = compressed.astype(BF16)


def basis_kernel(summed, inv, out):
    width = summed.shape[2]
    scale = jnp.sqrt(F32(NX * width))
    for x, block in enumerate(basis_blocks(summed, inv[...])):
        out[pl.ds(x * width, width), :] = (block * scale).T


def call(body, out_shape, operands, in_hbm, scratch, cost=None):
    spec = [pl.BlockSpec(memory_space=pl.ANY if h else pltpu.VMEM) for h in in_hbm]
    return pl.pallas_call(
        body,
        out_shape=out_shape,
        in_specs=spec,
        out_specs=jax.tree.map(lambda _: pl.BlockSpec(memory_space=pltpu.VMEM), out_shape),
        scratch_shapes=scratch,
        cost_estimate=cost,
        compiler_params=pltpu.CompilerParams(vmem_limit_bytes=VMEM_BYTES),
    )(*operands)


def add_up(terms):
    terms = [terms[i].astype(F32) for i in range(terms.shape[0])]
    while len(terms) > 1:
        terms = [a + b for a, b in zip(terms[0::2], terms[1::2])]
    return terms[0].astype(BF16)


def sum_and_spread(local_term):
    _, rank, width = local_term.shape
    near = NX * NZ_LOW
    part = rank // NZ_LOW
    terms = local_term.reshape(near, part, width)
    own = add_up(lax.all_to_all(terms, ("x", "z_low"), 0, 0, tiled=True))
    first, second, third = (
        lax.ppermute(own, "z_high", [(i, (i + step) % NZ_HIGH) for i in range(NZ_HIGH)]).astype(F32)
        for step in range(1, NZ_HIGH)
    )
    total = ((own.astype(F32) + second) + (first + third)).astype(BF16)
    total = jnp.broadcast_to(total[None], (near, part, width))
    blocks = lax.all_to_all(total, ("x", "z_low"), 0, 0, tiled=True)
    return blocks.reshape(NX, rank, width)


def local(key_cache, init_basis):
    positions, features = key_cache.shape
    rank = init_basis.shape[1]
    width = features // NX
    shape = jax.ShapeDtypeStruct
    square = pltpu.VMEM((rank, rank), F32)
    keys = pltpu.VMEM((positions, features), BF16)
    sem = pltpu.SemaphoreType.DMA
    blocks = shape((NX, rank, width), BF16)

    scratch = [keys, pltpu.VMEM((features, rank), F32), sem((NX,)), sem((NX,))]
    term = call(first_kernel, blocks, (key_cache, init_basis), (True, True), scratch)
    for sweep in range(ITERS - 1):
        summed = sum_and_spread(term)
        scratch = [square, square, keys, sem]
        term = call(middle_kernel, blocks, (summed, key_cache), (False, True), scratch)
    summed = sum_and_spread(term)
    outs = (shape((rank, rank), F32), shape((positions, rank), BF16))
    inv, compressed = call(
        last_kernel, outs, (summed, key_cache), (False, True), [square, keys, sem]
    )
    latents = lax.all_to_all(
        compressed, ("x", "z_high", "z_low"), split_axis=0, concat_axis=0, tiled=True
    )
    cost = pl.CostEstimate(
        flops=4 * rank * rank * features, bytes_accessed=8 * features * rank, transcendentals=0
    )
    basis = call(basis_kernel, shape((features, rank), F32), (summed, inv), (False, False), [], cost)
    return basis, latents


def solution(mesh):
    grid = Mesh(mesh.devices.reshape(NX, NZ_HIGH, NZ_LOW, -1), AXES)
    return jax.shard_map(
        local,
        mesh=grid,
        in_specs=(P(("grp",) + AXES[:3], None), P("grp", None)),
        out_specs=(P("grp", None), P(("grp",) + AXES[:3], None)),
        check_vma=False,
    )
```

```python
import jax
import jax.numpy as jnp
from jax import lax
from jax.experimental import pallas as pl
from jax.experimental.pallas import tpu as pltpu
from jax.sharding import Mesh
from jax.sharding import PartitionSpec as P

ITERS = 3
NX = 4
NZ_HIGH = 4
NZ_LOW = 2
NB = 32
GROUP = 8
CHUNKS = 4
STRIP = 16
NZ = NZ_HIGH * NZ_LOW
AXES = ("x", "z_high", "z_low", "grp")
POS = AXES[:3]
NEAR = [
    [x * NZ + 2 * high + (low ^ (high % 2)) for x in range(NX) for low in range(NZ_LOW)]
    for high in range(NZ_HIGH)
]
PAIRS = (((1, 2), (3, 4), (5, 6), (7, 0)), ((0, 3), (2, 5), (4, 7), (6, 1)))
VMEM_BYTES = 54_000_000
F32 = jnp.float32
BF16 = jnp.bfloat16

NN = (((1,), (0,)), ((), ()))
NT = (((1,), (1,)), ((), ()))
TN = (((0,), (0,)), ((), ()))


def dot(a, b, dims):
    return lax.dot_general(a, b, dims, preferred_element_type=F32)


def split(a):
    high = a.astype(BF16)
    rest = a - high.astype(F32)
    mid = rest.astype(BF16)
    low = (rest - mid.astype(F32)).astype(BF16)
    return high, mid, low


def stacked(parts, order):
    return jnp.concatenate([parts[i] for i in order], axis=0)


LEFT = (0, 0, 1, 0, 2, 1)
RIGHT = (0, 1, 0, 2, 0, 1)


def widen(a, lanes):
    return jnp.concatenate([a] * (lanes // 128), axis=1) if lanes > 128 else a


def eliminate(rows, inverse, column):
    row_id = lax.broadcasted_iota(jnp.int32, (GROUP, 128), 0)
    groups = len(rows)
    rows, inverse = list(rows), list(inverse)
    lanes, inverse_lanes = rows[0].shape[1], inverse[0].shape[1]
    for first in range(0, groups, STRIP // GROUP):
        held = {}
        for g in range(first, groups):
            at = column + first * GROUP
            held[g] = [
                jnp.broadcast_to(rows[g][:, at + s : at + s + 1], (GROUP, 128)) for s in range(STRIP)
            ]
        for s in range(STRIP):
            own, k = first + s // GROUP, s % GROUP
            if k == 0:
                pivots = jnp.ones((GROUP, 128), F32)
            pivot = held[own][s][k : k + 1, :]
            reciprocal = 1.0 / pivot
            pivots = jnp.where(row_id == k, pivot, pivots)
            heads = [held[own][t][k : k + 1, :] * reciprocal for t in range(s + 1, STRIP)]
            pivot_row, pivot_inverse = rows[own][k : k + 1, :], inverse[own][k : k + 1, :]
            for g in range(own, groups):
                base = held[g][s]
                for t in range(s + 1, STRIP):
                    held[g][t] = held[g][t] - base * heads[t - s - 1]
                factor = base * reciprocal
                if g == own:
                    factor = jnp.where(row_id > k, factor, 0.0)
                rows[g] = rows[g] - widen(factor, lanes) * pivot_row
                inverse[g] = inverse[g] - widen(factor, inverse_lanes) * pivot_inverse
            if k == GROUP - 1:
                scale = lax.rsqrt(pivots)
                rows[own] = rows[own] * widen(scale, lanes)
                inverse[own] = inverse[own] * widen(scale, inverse_lanes)
    return rows, inverse


def inverse_factor(gram, inv, beside):
    n = gram.shape[0]
    eye = lax.broadcasted_iota(jnp.int32, (n, n), 0) == lax.broadcasted_iota(jnp.int32, (n, n), 1)
    inv[...] = eye.astype(F32)
    for start in range(0, n, NB):
        done = start + NB
        left = start // 128 * 128
        right = -(-done // 128) * 128
        groups = [pl.ds(start + g, GROUP) for g in range(0, NB, GROUP)]
        beside(start // NB)
        upper, lower = eliminate(
            [gram[g, left:] for g in groups], [inv[g, :right] for g in groups], start - left
        )
        upper, lower = jnp.concatenate(upper, axis=0), jnp.concatenate(lower, axis=0)
        inv[pl.ds(start, NB), :right] = lower
        if done < n:
            keep = done // 128 * 128
            upper_parts = split(upper[:, keep - left :])
            factor = stacked(upper_parts, LEFT)
            rest = pl.ds(done, n - done)
            update = dot(factor, stacked(upper_parts, RIGHT), TN)
            gram[rest, keep:] = gram[rest, keep:] - update[done - keep :]
            update = dot(factor, stacked(split(lower), RIGHT), TN)
            inv[rest, :right] = inv[rest, :right] - update[done - keep :]


def first_kernel(keys_hbm, basis_hbm, out, keys, basis, key_sems, basis_sems):
    width = keys.shape[1] // NX
    copies = []
    for x in range(NX):
        part = pl.ds(x * width, width)
        of_basis = pltpu.make_async_copy(basis_hbm.at[part, :], basis.at[part, :], basis_sems.at[x])
        of_keys = pltpu.make_async_copy(keys_hbm.at[:, part], keys.at[:, part], key_sems.at[x])
        of_basis.start()
        of_keys.start()
        copies.append((of_basis, of_keys))
    projected = 0.0
    for x, (of_basis, of_keys) in enumerate(copies):
        of_basis.wait()
        rounded = basis[pl.ds(x * width, width), :].T.astype(BF16)
        of_keys.wait()
        projected = projected + dot(rounded, keys[:, x * width : (x + 1) * width], NT)
    projected = projected.astype(BF16)
    for x in range(NX):
        out[x] = dot(projected, keys[:, x * width : (x + 1) * width], NN).astype(BF16)


def basis_blocks(summed, inv):
    high, mid, _ = split(inv)
    return [dot(high, summed[x], NN) + dot(mid, summed[x], NN) for x in range(NX)]


def factorize(summed, gram, inv, multiply):
    total = 0.0
    for x in range(NX):
        total = total + dot(summed[x], summed[x], NT)
    gram[...] = total
    blocks = gram.shape[0] // NB

    def beside(block):
        if block >= blocks - CHUNKS:
            multiply(block - (blocks - CHUNKS))

    inverse_factor(gram, inv, beside)


def two_part(a):
    high, mid, _ = split(a)
    return high, mid


def three_products(a, b, dims):
    (a_high, a_mid), (b_high, b_mid) = two_part(a), two_part(b)
    return dot(a_high, b_high, dims) + dot(a_high, b_mid, dims) + dot(a_mid, b_high, dims)


def middle_kernel(summed, keys_hbm, out, gram, inv, mixed, keys, sem):
    copy = pltpu.make_async_copy(keys_hbm, keys, sem)
    copy.start()
    width = summed.shape[2]
    size = keys.shape[0] // CHUNKS

    def multiply(chunk):
        if chunk == 0:
            copy.wait()
        at = chunk * size
        total = 0.0
        for x in range(NX):
            total = total + dot(summed[x], keys[at : at + size, x * width : (x + 1) * width], NT)
        mixed[:, at : at + size] = total

    factorize(summed, gram, inv, multiply)
    projected = three_products(inv[...], mixed[...], NN).astype(BF16)
    for x in range(NX):
        out[x] = dot(projected, keys[:, x * width : (x + 1) * width], NN).astype(BF16)


def last_kernel(summed, keys_hbm, inv, out, gram, mixed, keys, sem):
    copy = pltpu.make_async_copy(keys_hbm, keys, sem)
    copy.start()
    width = summed.shape[2]
    size = keys.shape[0] // CHUNKS

    def multiply(chunk):
        if chunk == 0:
            copy.wait()
        at = chunk * size
        total = 0.0
        for x in range(NX):
            total = total + dot(keys[at : at + size, x * width : (x + 1) * width], summed[x], NT)
        mixed[at : at + size, :] = total

    factorize(summed, gram, inv, multiply)
    out[...] = three_products(mixed[...], inv[...], NT).astype(BF16)


def basis_kernel(summed, inv, out):
    width = summed.shape[2]
    scale = jnp.sqrt(F32(NX * width))
    for x, block in enumerate(basis_blocks(summed, inv[...])):
        out[pl.ds(x * width, width), :] = (block * scale).T


def call(body, out_shape, operands, in_hbm, scratch, cost=None):
    spec = [pl.BlockSpec(memory_space=pltpu.HBM if h else pltpu.VMEM) for h in in_hbm]
    return pl.pallas_call(
        body,
        out_shape=out_shape,
        in_specs=spec,
        out_specs=jax.tree.map(lambda _: pl.BlockSpec(memory_space=pltpu.VMEM), out_shape),
        scratch_shapes=scratch,
        cost_estimate=cost,
        compiler_params=pltpu.CompilerParams(vmem_limit_bytes=VMEM_BYTES),
    )(*operands)


def add_up(terms):
    terms = [terms[i].astype(F32) for i in range(terms.shape[0])]
    while len(terms) > 1:
        terms = [a + b for a, b in zip(terms[0::2], terms[1::2])]
    return terms[0].astype(BF16)


def sum_and_spread(local_term):
    _, rank, width = local_term.shape
    near = NX * NZ_LOW
    part = rank // NZ_LOW
    terms = local_term.reshape(near, part, width)
    own = add_up(lax.all_to_all(terms, POS, 0, 0, axis_index_groups=NEAR, tiled=True))
    for pairs in PAIRS:
        both_ways = [
            (x * NZ + p, x * NZ + q) for x in range(NX) for a, b in pairs for p, q in ((a, b), (b, a))
        ]
        own = (own.astype(F32) + lax.ppermute(own, POS, both_ways).astype(F32)).astype(BF16)
    total = own
    total = jnp.broadcast_to(total[None], (near, part, width))
    blocks = lax.all_to_all(total, POS, 0, 0, axis_index_groups=NEAR, tiled=True)
    return blocks.reshape(NX, rank, width)


def local(key_cache, init_basis):
    positions, features = key_cache.shape
    rank = init_basis.shape[1]
    width = features // NX
    shape = jax.ShapeDtypeStruct
    square = pltpu.VMEM((rank, rank), F32)
    keys = pltpu.VMEM((positions, features), BF16)
    sem = pltpu.SemaphoreType.DMA
    blocks = shape((NX, rank, width), BF16)

    scratch = [keys, pltpu.VMEM((features, rank), F32), sem((NX,)), sem((NX,))]
    term = call(first_kernel, blocks, (key_cache, init_basis), (True, True), scratch)
    for sweep in range(ITERS - 1):
        summed = sum_and_spread(term)
        scratch = [square, square, pltpu.VMEM((rank, positions), F32), keys, sem]
        term = call(middle_kernel, blocks, (summed, key_cache), (False, True), scratch)
    summed = sum_and_spread(term)
    outs = (shape((rank, rank), F32), shape((positions, rank), BF16))
    scratch = [square, pltpu.VMEM((positions, rank), F32), keys, sem]
    inv, compressed = call(last_kernel, outs, (summed, key_cache), (False, True), scratch)
    latents = lax.all_to_all(
        compressed, ("x", "z_high", "z_low"), split_axis=0, concat_axis=0, tiled=True
    )
    cost = pl.CostEstimate(
        flops=4 * rank * rank * features, bytes_accessed=8 * features * rank, transcendentals=0
    )
    basis = call(basis_kernel, shape((features, rank), F32), (summed, inv), (False, False), [], cost)
    return basis, latents


def solution(mesh):
    grid = Mesh(mesh.devices.reshape(NX, NZ_HIGH, NZ_LOW, -1), AXES)
    return jax.shard_map(
        local,
        mesh=grid,
        in_specs=(P(("grp",) + AXES[:3], None), P("grp", None)),
        out_specs=(P("grp", None), P(("grp",) + AXES[:3], None)),
        check_vma=False,
    )
```

```python
import jax
import jax.numpy as jnp
from jax import lax
from jax.experimental import pallas as pl
from jax.experimental.pallas import tpu as pltpu
from jax.sharding import Mesh
from jax.sharding import PartitionSpec as P

ITERS = 3
NX = 4
NZ_HIGH = 4
NZ_LOW = 2
NB = 32
GROUP = 8
CHUNKS = 4
STRIP = 16
NZ = NZ_HIGH * NZ_LOW
AXES = ("x", "z_high", "z_low", "grp")
POS = AXES[:3]
NEAR = [
    [x * NZ + 2 * high + (low ^ (high % 2)) for x in range(NX) for low in range(NZ_LOW)]
    for high in range(NZ_HIGH)
]
PAIRS = (((0, 3), (2, 5), (4, 7), (6, 1)), ((1, 2), (3, 4), (5, 6), (7, 0)))
VMEM_BYTES = 54_000_000
F32 = jnp.float32
BF16 = jnp.bfloat16

TERMS = BF16
SUMS = F32
PARTS = 2

NN = (((1,), (0,)), ((), ()))
NT = (((1,), (1,)), ((), ()))
TN = (((0,), (0,)), ((), ()))


def dot(a, b, dims):
    return lax.dot_general(a, b, dims, preferred_element_type=F32)


def split(a):
    high = a.astype(BF16)
    rest = a - high.astype(F32)
    mid = rest.astype(BF16)
    low = (rest - mid.astype(F32)).astype(BF16)
    return high, mid, low


def stacked(parts, order):
    return jnp.concatenate([parts[i] for i in order], axis=0)


LEFT = (0, 0, 1, 0, 2, 1)
RIGHT = (0, 1, 0, 2, 0, 1)


def widen(a, lanes):
    return jnp.concatenate([a] * (lanes // 128), axis=1) if lanes > 128 else a


def eliminate(rows, inverse, column):
    row_id = lax.broadcasted_iota(jnp.int32, (GROUP, 128), 0)
    groups = len(rows)
    rows, inverse = list(rows), list(inverse)
    lanes, inverse_lanes = rows[0].shape[1], inverse[0].shape[1]
    for first in range(0, groups, STRIP // GROUP):
        held = {}
        for g in range(first, groups):
            at = column + first * GROUP
            held[g] = [
                jnp.broadcast_to(rows[g][:, at + s : at + s + 1], (GROUP, 128)) for s in range(STRIP)
            ]
        for s in range(STRIP):
            own, k = first + s // GROUP, s % GROUP
            if k == 0:
                pivots = jnp.ones((GROUP, 128), F32)
            pivot = held[own][s][k : k + 1, :]
            reciprocal = 1.0 / pivot
            pivots = jnp.where(row_id == k, pivot, pivots)
            heads = [held[own][t][k : k + 1, :] * reciprocal for t in range(s + 1, STRIP)]
            pivot_row, pivot_inverse = rows[own][k : k + 1, :], inverse[own][k : k + 1, :]
            for g in range(own, groups):
                base = held[g][s]
                for t in range(s + 1, STRIP):
                    held[g][t] = held[g][t] - base * heads[t - s - 1]
                factor = base * reciprocal
                if g == own:
                    factor = jnp.where(row_id > k, factor, 0.0)
                rows[g] = rows[g] - widen(factor, lanes) * pivot_row
                inverse[g] = inverse[g] - widen(factor, inverse_lanes) * pivot_inverse
            if k == GROUP - 1:
                scale = lax.rsqrt(pivots)
                rows[own] = rows[own] * widen(scale, lanes)
                inverse[own] = inverse[own] * widen(scale, inverse_lanes)
    return rows, inverse


def inverse_factor(gram, inv, beside):
    n = gram.shape[0]
    eye = lax.broadcasted_iota(jnp.int32, (n, n), 0) == lax.broadcasted_iota(jnp.int32, (n, n), 1)
    inv[...] = eye.astype(F32)
    for start in range(0, n, NB):
        done = start + NB
        left = start // 128 * 128
        right = -(-done // 128) * 128
        groups = [pl.ds(start + g, GROUP) for g in range(0, NB, GROUP)]
        beside(start // NB)
        upper, lower = eliminate(
            [gram[g, left:] for g in groups], [inv[g, :right] for g in groups], start - left
        )
        upper, lower = jnp.concatenate(upper, axis=0), jnp.concatenate(lower, axis=0)
        inv[pl.ds(start, NB), :right] = lower
        if done < n:
            keep = done // 128 * 128
            upper_parts = split(upper[:, keep - left :])
            factor = stacked(upper_parts, LEFT)
            rest = pl.ds(done, n - done)
            update = dot(factor, stacked(upper_parts, RIGHT), TN)
            gram[rest, keep:] = gram[rest, keep:] - update[done - keep :]
            update = dot(factor, stacked(split(lower), RIGHT), TN)
            inv[rest, :right] = inv[rest, :right] - update[done - keep :]


def first_kernel(keys_hbm, basis_hbm, out, keys, basis, key_sems, basis_sems):
    width = keys.shape[1] // NX
    copies = []
    for x in range(NX):
        part = pl.ds(x * width, width)
        of_basis = pltpu.make_async_copy(basis_hbm.at[part, :], basis.at[part, :], basis_sems.at[x])
        of_keys = pltpu.make_async_copy(keys_hbm.at[:, part], keys.at[:, part], key_sems.at[x])
        of_basis.start()
        of_keys.start()
        copies.append((of_basis, of_keys))
    projected = 0.0
    for x, (of_basis, of_keys) in enumerate(copies):
        of_basis.wait()
        rounded = basis[pl.ds(x * width, width), :].T.astype(BF16)
        of_keys.wait()
        projected = projected + dot(rounded, keys[:, x * width : (x + 1) * width], NT)
    projected = projected.astype(BF16)
    for x in range(NX):
        out[x] = dot(projected, keys[:, x * width : (x + 1) * width], NN).astype(out.dtype)


def basis_blocks(summed, inv):
    high, mid, _ = split(inv)
    return [dot(high, summed[x], NN) + dot(mid, summed[x], NN) for x in range(NX)]


def factorize(summed, gram, inv, multiply):
    total = 0.0
    for x in range(NX):
        total = total + dot(summed[x], summed[x], NT)
    gram[...] = total
    blocks = gram.shape[0] // NB

    def beside(block):
        if block >= blocks - CHUNKS:
            multiply(block - (blocks - CHUNKS))

    inverse_factor(gram, inv, beside)


def two_part(a):
    high, mid, _ = split(a)
    return high, mid


def three_products(a, b, dims):
    (a_high, a_mid), (b_high, b_mid) = two_part(a), two_part(b)
    return dot(a_high, b_high, dims) + dot(a_high, b_mid, dims) + dot(a_mid, b_high, dims)


def middle_kernel(blocks, keys_hbm, out, gram, inv, mixed, keys, sem):
    copy = pltpu.make_async_copy(keys_hbm, keys, sem)
    copy.start()
    width = blocks.shape[4]
    size = keys.shape[0] // CHUNKS
    parts = [
        [jnp.concatenate([blocks[x, z, p] for z in range(NZ_LOW)], axis=0) for x in range(NX)]
        for p in range(blocks.shape[2])
    ]

    def multiply(chunk):
        if chunk == 0:
            copy.wait()
        at = chunk * size
        total = 0.0
        for part in parts:
            for x in range(NX):
                total = total + dot(part[x], keys[at : at + size, x * width : (x + 1) * width], NT)
        mixed[:, at : at + size] = total

    factorize(parts[0], gram, inv, multiply)
    projected = three_products(inv[...], mixed[...], NN).astype(BF16)
    for x in range(NX):
        out[x] = dot(projected, keys[:, x * width : (x + 1) * width], NN).astype(out.dtype)


def last_kernel(summed, keys_hbm, inv, out, gram, mixed, keys, sem):
    copy = pltpu.make_async_copy(keys_hbm, keys, sem)
    copy.start()
    width = summed.shape[2]
    size = keys.shape[0] // CHUNKS

    def multiply(chunk):
        if chunk == 0:
            copy.wait()
        at = chunk * size
        total = 0.0
        for x in range(NX):
            total = total + dot(keys[at : at + size, x * width : (x + 1) * width], summed[x], NT)
        mixed[at : at + size, :] = total

    factorize(summed, gram, inv, multiply)
    out[...] = three_products(mixed[...], inv[...], NT).astype(BF16)


def basis_kernel(summed, inv, out):
    width = summed.shape[2]
    scale = jnp.sqrt(F32(NX * width))
    for x, block in enumerate(basis_blocks(summed, inv[...])):
        out[pl.ds(x * width, width), :] = (block * scale).T


def call(body, out_shape, operands, in_hbm, scratch, cost=None):
    spec = [pl.BlockSpec(memory_space=pltpu.HBM if h else pltpu.VMEM) for h in in_hbm]
    return pl.pallas_call(
        body,
        out_shape=out_shape,
        in_specs=spec,
        out_specs=jax.tree.map(lambda _: pl.BlockSpec(memory_space=pltpu.VMEM), out_shape),
        scratch_shapes=scratch,
        cost_estimate=cost,
        compiler_params=pltpu.CompilerParams(vmem_limit_bytes=VMEM_BYTES),
    )(*operands)


def add_up(terms):
    terms = [terms[i].astype(F32) for i in range(terms.shape[0])]
    while len(terms) > 1:
        terms = [a + b for a, b in zip(terms[0::2], terms[1::2])]
    return terms[0]


def sum_and_spread(local_term, sums, parts):
    _, rank, width = local_term.shape
    near = NX * NZ_LOW
    part = rank // NZ_LOW
    terms = local_term.reshape(near, part, width)
    terms = lax.all_to_all(terms, POS, 0, 0, axis_index_groups=NEAR, tiled=True)
    own = add_up(terms).astype(sums)
    for pairs in PAIRS:
        both_ways = [
            (x * NZ + p, x * NZ + q) for x in range(NX) for a, b in pairs for p, q in ((a, b), (b, a))
        ]
        other = lax.ppermute(own, POS, both_ways)
        own = (own.astype(F32) + other.astype(F32)).astype(sums)
    total = jnp.stack(split(own.astype(F32))[:parts]) if parts > 1 else own.astype(BF16)[None]
    total = jnp.broadcast_to(total[None], (near, parts, part, width))
    blocks = lax.all_to_all(total, POS, 0, 0, axis_index_groups=NEAR, tiled=True)
    return blocks.reshape(NX, NZ_LOW, parts, part, width)


def local(key_cache, init_basis):
    positions, features = key_cache.shape
    rank = init_basis.shape[1]
    width = features // NX
    shape = jax.ShapeDtypeStruct
    square = pltpu.VMEM((rank, rank), F32)
    keys = pltpu.VMEM((positions, features), BF16)
    sem = pltpu.SemaphoreType.DMA
    blocks = shape((NX, rank, width), BF16)

    scratch = [keys, pltpu.VMEM((features, rank), F32), sem((NX,)), sem((NX,))]
    term = call(first_kernel, shape((NX, rank, width), TERMS), (key_cache, init_basis), (True, True), scratch)
    for sweep in range(ITERS - 1):
        summed = sum_and_spread(term, *((SUMS, PARTS) if sweep == 0 else (BF16, 1)))
        scratch = [square, square, pltpu.VMEM((rank, positions), F32), keys, sem]
        term = call(middle_kernel, blocks, (summed, key_cache), (False, True), scratch)
    summed = sum_and_spread(term, BF16, 1).reshape(NX, rank, width)
    outs = (shape((rank, rank), F32), shape((positions, rank), BF16))
    scratch = [square, pltpu.VMEM((positions, rank), F32), keys, sem]
    inv, compressed = call(last_kernel, outs, (summed, key_cache), (False, True), scratch)
    latents = lax.all_to_all(
        compressed, ("x", "z_high", "z_low"), split_axis=0, concat_axis=0, tiled=True
    )
    cost = pl.CostEstimate(
        flops=4 * rank * rank * features, bytes_accessed=8 * features * rank, transcendentals=0
    )
    basis = call(basis_kernel, shape((features, rank), F32), (summed, inv), (False, False), [], cost)
    return basis, latents


def solution(mesh):
    grid = Mesh(mesh.devices.reshape(NX, NZ_HIGH, NZ_LOW, -1), AXES)
    return jax.shard_map(
        local,
        mesh=grid,
        in_specs=(P(("grp",) + AXES[:3], None), P("grp", None)),
        out_specs=(P("grp", None), P(("grp",) + AXES[:3], None)),
        check_vma=False,
    )
```

```python
import jax
import jax.numpy as jnp
from jax import lax
from jax.experimental import pallas as pl
from jax.experimental.pallas import tpu as pltpu
from jax.sharding import Mesh
from jax.sharding import PartitionSpec as P

ITERS = 3
NX = 4
NZ_HIGH = 4
NZ_LOW = 2
NB = 32
GROUP = 8
CHUNKS = 4
STRIP = 16
NZ = NZ_HIGH * NZ_LOW
AXES = ("x", "z_high", "z_low", "grp")
POS = AXES[:3]
NEAR = [
    [x * NZ + 2 * high + (low ^ (high % 2)) for low in range(NZ_LOW) for x in range(NX)]
    for high in range(NZ_HIGH)
]
PAIRS = (((0, 3), (2, 5), (4, 7), (6, 1)), ((1, 2), (3, 4), (5, 6), (7, 0)))
VMEM_BYTES = 54_000_000
F32 = jnp.float32
BF16 = jnp.bfloat16

TERMS = BF16
SUMS = BF16
PARTS = 1

NN = (((1,), (0,)), ((), ()))
NT = (((1,), (1,)), ((), ()))
TN = (((0,), (0,)), ((), ()))


def dot(a, b, dims):
    return lax.dot_general(a, b, dims, preferred_element_type=F32)


def split(a):
    high = a.astype(BF16)
    rest = a - high.astype(F32)
    mid = rest.astype(BF16)
    low = (rest - mid.astype(F32)).astype(BF16)
    return high, mid, low


def stacked(parts, order):
    return jnp.concatenate([parts[i] for i in order], axis=0)


LEFT = (0, 0, 1, 0, 2, 1)
RIGHT = (0, 1, 0, 2, 0, 1)


def widen(a, lanes):
    return jnp.concatenate([a] * (lanes // 128), axis=1) if lanes > 128 else a


def eliminate(rows, inverse, column):
    row_id = lax.broadcasted_iota(jnp.int32, (GROUP, 128), 0)
    groups = len(rows)
    rows, inverse = list(rows), list(inverse)
    lanes, inverse_lanes = rows[0].shape[1], inverse[0].shape[1]
    for first in range(0, groups, STRIP // GROUP):
        held = {}
        for g in range(first, groups):
            at = column + first * GROUP
            held[g] = [
                jnp.broadcast_to(rows[g][:, at + s : at + s + 1], (GROUP, 128)) for s in range(STRIP)
            ]
        for s in range(STRIP):
            own, k = first + s // GROUP, s % GROUP
            if k == 0:
                pivots = jnp.ones((GROUP, 128), F32)
            pivot = held[own][s][k : k + 1, :]
            reciprocal = 1.0 / pivot
            pivots = jnp.where(row_id == k, pivot, pivots)
            heads = [held[own][t][k : k + 1, :] * reciprocal for t in range(s + 1, STRIP)]
            pivot_row, pivot_inverse = rows[own][k : k + 1, :], inverse[own][k : k + 1, :]
            for g in range(own, groups):
                base = held[g][s]
                for t in range(s + 1, STRIP):
                    held[g][t] = held[g][t] - base * heads[t - s - 1]
                factor = base * reciprocal
                if g == own:
                    factor = jnp.where(row_id > k, factor, 0.0)
                rows[g] = rows[g] - widen(factor, lanes) * pivot_row
                inverse[g] = inverse[g] - widen(factor, inverse_lanes) * pivot_inverse
            if k == GROUP - 1:
                scale = lax.rsqrt(pivots)
                rows[own] = rows[own] * widen(scale, lanes)
                inverse[own] = inverse[own] * widen(scale, inverse_lanes)
    return rows, inverse


def inverse_factor(gram, inv, beside):
    n = gram.shape[0]
    eye = lax.broadcasted_iota(jnp.int32, (n, n), 0) == lax.broadcasted_iota(jnp.int32, (n, n), 1)
    inv[...] = eye.astype(F32)
    for start in range(0, n, NB):
        done = start + NB
        left = start // 128 * 128
        right = -(-done // 128) * 128
        groups = [pl.ds(start + g, GROUP) for g in range(0, NB, GROUP)]
        beside(start // NB)
        upper, lower = eliminate(
            [gram[g, left:] for g in groups], [inv[g, :right] for g in groups], start - left
        )
        upper, lower = jnp.concatenate(upper, axis=0), jnp.concatenate(lower, axis=0)
        inv[pl.ds(start, NB), :right] = lower
        if done < n:
            keep = done // 128 * 128
            upper_parts = split(upper[:, keep - left :])
            factor = stacked(upper_parts, LEFT)
            rest = pl.ds(done, n - done)
            update = dot(factor, stacked(upper_parts, RIGHT), TN)
            gram[rest, keep:] = gram[rest, keep:] - update[done - keep :]
            update = dot(factor, stacked(split(lower), RIGHT), TN)
            inv[rest, :right] = inv[rest, :right] - update[done - keep :]


def first_kernel(keys_hbm, basis_hbm, out, keys, basis, key_sems, basis_sems):
    width = keys.shape[1] // NX
    copies = []
    for x in range(NX):
        part = pl.ds(x * width, width)
        of_basis = pltpu.make_async_copy(basis_hbm.at[part, :], basis.at[part, :], basis_sems.at[x])
        of_keys = pltpu.make_async_copy(keys_hbm.at[:, part], keys.at[:, part], key_sems.at[x])
        of_basis.start()
        of_keys.start()
        copies.append((of_basis, of_keys))
    projected = 0.0
    for x, (of_basis, of_keys) in enumerate(copies):
        of_basis.wait()
        rounded = basis[pl.ds(x * width, width), :].T.astype(BF16)
        of_keys.wait()
        projected = projected + dot(rounded, keys[:, x * width : (x + 1) * width], NT)
    projected = projected.astype(BF16)
    for x in range(NX):
        out[x] = dot(projected, keys[:, x * width : (x + 1) * width], NN).astype(out.dtype)


def basis_blocks(summed, inv):
    high, mid, _ = split(inv)
    return [dot(high, summed[x], NN) + dot(mid, summed[x], NN) for x in range(NX)]


def factorize(summed, gram, inv, multiply):
    total = 0.0
    for x in range(NX):
        total = total + dot(summed[x], summed[x], NT)
    gram[...] = total
    blocks = gram.shape[0] // NB

    def beside(block):
        if block >= blocks - CHUNKS:
            multiply(block - (blocks - CHUNKS))

    inverse_factor(gram, inv, beside)


def two_part(a):
    high, mid, _ = split(a)
    return high, mid


def three_products(a, b, dims):
    (a_high, a_mid), (b_high, b_mid) = two_part(a), two_part(b)
    return dot(a_high, b_high, dims) + dot(a_high, b_mid, dims) + dot(a_mid, b_high, dims)


def middle_kernel(blocks, keys_hbm, out, gram, inv, mixed, keys, sem):
    copy = pltpu.make_async_copy(keys_hbm, keys, sem)
    copy.start()
    width = blocks.shape[4]
    size = keys.shape[0] // CHUNKS
    parts = [
        [jnp.concatenate([blocks[x, z, p] for z in range(NZ_LOW)], axis=0) for x in range(NX)]
        for p in range(blocks.shape[2])
    ]

    def multiply(chunk):
        if chunk == 0:
            copy.wait()
        at = chunk * size
        total = 0.0
        for part in parts:
            for x in range(NX):
                total = total + dot(part[x], keys[at : at + size, x * width : (x + 1) * width], NT)
        mixed[:, at : at + size] = total

    factorize(parts[0], gram, inv, multiply)
    projected = three_products(inv[...], mixed[...], NN).astype(BF16)
    for x in range(NX):
        out[x] = dot(projected, keys[:, x * width : (x + 1) * width], NN).astype(out.dtype)


def last_kernel(summed, keys_hbm, inv, out, gram, mixed, keys, sem):
    copy = pltpu.make_async_copy(keys_hbm, keys, sem)
    copy.start()
    width = summed.shape[2]
    size = keys.shape[0] // CHUNKS

    def multiply(chunk):
        if chunk == 0:
            copy.wait()
        at = chunk * size
        total = 0.0
        for x in range(NX):
            total = total + dot(keys[at : at + size, x * width : (x + 1) * width], summed[x], NT)
        mixed[at : at + size, :] = total

    factorize(summed, gram, inv, multiply)
    out[...] = three_products(mixed[...], inv[...], NT).astype(BF16)


def basis_kernel(summed, inv, out):
    width = summed.shape[2]
    scale = jnp.sqrt(F32(NX * width))
    for x, block in enumerate(basis_blocks(summed, inv[...])):
        out[pl.ds(x * width, width), :] = (block * scale).T


def call(body, out_shape, operands, in_hbm, scratch, cost=None):
    spec = [pl.BlockSpec(memory_space=pltpu.HBM if h else pltpu.VMEM) for h in in_hbm]
    return pl.pallas_call(
        body,
        out_shape=out_shape,
        in_specs=spec,
        out_specs=jax.tree.map(lambda _: pl.BlockSpec(memory_space=pltpu.VMEM), out_shape),
        scratch_shapes=scratch,
        cost_estimate=cost,
        compiler_params=pltpu.CompilerParams(vmem_limit_bytes=VMEM_BYTES),
    )(*operands)


def add_up(terms):
    terms = [terms[i].astype(F32) for i in range(terms.shape[0])]
    while len(terms) > 1:
        terms = [a + b for a, b in zip(terms[0::2], terms[1::2])]
    return terms[0]


def sum_and_spread(local_term, sums, parts):
    _, rank, width = local_term.shape
    near = NX * NZ_LOW
    part = rank // NZ_LOW
    terms = local_term.reshape(near, part, width)
    terms = lax.all_to_all(terms, POS, 0, 0, axis_index_groups=NEAR, tiled=True)
    own = add_up(terms).astype(sums)
    for pairs in PAIRS:
        both_ways = [
            (x * NZ + p, x * NZ + q) for x in range(NX) for a, b in pairs for p, q in ((a, b), (b, a))
        ]
        other = lax.ppermute(own, POS, both_ways)
        own = (own.astype(F32) + other.astype(F32)).astype(sums)
    total = jnp.stack(split(own.astype(F32))[:parts]) if parts > 1 else own.astype(BF16)[None]
    total = jnp.broadcast_to(total[None], (near, parts, part, width))
    blocks = lax.all_to_all(total, POS, 0, 0, axis_index_groups=NEAR, tiled=True)
    return blocks.reshape(NX, NZ_LOW, parts, part, width)


def local(key_cache, init_basis):
    positions, features = key_cache.shape
    rank = init_basis.shape[1]
    width = features // NX
    shape = jax.ShapeDtypeStruct
    square = pltpu.VMEM((rank, rank), F32)
    keys = pltpu.VMEM((positions, features), BF16)
    sem = pltpu.SemaphoreType.DMA
    blocks = shape((NX, rank, width), BF16)

    scratch = [keys, pltpu.VMEM((features, rank), F32), sem((NX,)), sem((NX,))]
    term = call(first_kernel, shape((NX, rank, width), TERMS), (key_cache, init_basis), (True, True), scratch)
    for sweep in range(ITERS - 1):
        summed = sum_and_spread(term, *((SUMS, PARTS) if sweep == 0 else (BF16, 1)))
        scratch = [square, square, pltpu.VMEM((rank, positions), F32), keys, sem]
        term = call(middle_kernel, blocks, (summed, key_cache), (False, True), scratch)
    summed = sum_and_spread(term, BF16, 1).reshape(NX, rank, width)
    outs = (shape((rank, rank), F32), shape((positions, rank), BF16))
    scratch = [square, pltpu.VMEM((positions, rank), F32), keys, sem]
    inv, compressed = call(last_kernel, outs, (summed, key_cache), (False, True), scratch)
    latents = lax.all_to_all(
        compressed, ("x", "z_high", "z_low"), split_axis=0, concat_axis=0, tiled=True
    )
    cost = pl.CostEstimate(
        flops=4 * rank * rank * features, bytes_accessed=8 * features * rank, transcendentals=0
    )
    basis = call(basis_kernel, shape((features, rank), F32), (summed, inv), (False, False), [], cost)
    return basis, latents


def solution(mesh):
    grid = Mesh(mesh.devices.reshape(NX, NZ_HIGH, NZ_LOW, -1), AXES)
    return jax.shard_map(
        local,
        mesh=grid,
        in_specs=(P(("grp",) + AXES[:3], None), P("grp", None)),
        out_specs=(P("grp", None), P(("grp",) + AXES[:3], None)),
        check_vma=False,
    )
```

```python
import jax
import jax.numpy as jnp
from jax import lax
from jax.experimental import pallas as pl
from jax.experimental.pallas import tpu as pltpu
from jax.sharding import Mesh
from jax.sharding import PartitionSpec as P

ITERS = 3
NX = 4
NZ_HIGH = 4
NZ_LOW = 2
NB = 32
GROUP = 8
CHUNKS = 4
STRIP = 16
NZ = NZ_HIGH * NZ_LOW
AXES = ("x", "z_high", "z_low", "grp")
POS = AXES[:3]
NEAR = [
    [x * NZ + 2 * high + (low ^ (high % 2)) for low in range(NZ_LOW) for x in range(NX)]
    for high in range(NZ_HIGH)
]
PAIRS = (((0, 3), (2, 5), (4, 7), (6, 1)), ((1, 2), (3, 4), (5, 6), (7, 0)))
VMEM_BYTES = 54_000_000
F32 = jnp.float32
BF16 = jnp.bfloat16

SUMS = F32
PARTS = 2

NN = (((1,), (0,)), ((), ()))
NT = (((1,), (1,)), ((), ()))
TN = (((0,), (0,)), ((), ()))


def dot(a, b, dims):
    return lax.dot_general(a, b, dims, preferred_element_type=F32)


def split(a):
    high = a.astype(BF16)
    rest = a - high.astype(F32)
    mid = rest.astype(BF16)
    low = (rest - mid.astype(F32)).astype(BF16)
    return high, mid, low


def stacked(parts, order):
    return jnp.concatenate([parts[i] for i in order], axis=0)


LEFT = (0, 0, 1, 0, 2, 1)
RIGHT = (0, 1, 0, 2, 0, 1)


def widen(a, lanes):
    return jnp.concatenate([a] * (lanes // 128), axis=1) if lanes > 128 else a


def eliminate(rows, inverse, column):
    row_id = lax.broadcasted_iota(jnp.int32, (GROUP, 128), 0)
    groups = len(rows)
    rows, inverse = list(rows), list(inverse)
    lanes, inverse_lanes = rows[0].shape[1], inverse[0].shape[1]
    for first in range(0, groups, STRIP // GROUP):
        held = {}
        for g in range(first, groups):
            at = column + first * GROUP
            held[g] = [
                jnp.broadcast_to(rows[g][:, at + s : at + s + 1], (GROUP, 128)) for s in range(STRIP)
            ]
        for s in range(STRIP):
            own, k = first + s // GROUP, s % GROUP
            if k == 0:
                pivots = jnp.ones((GROUP, 128), F32)
            pivot = held[own][s][k : k + 1, :]
            reciprocal = 1.0 / pivot
            pivots = jnp.where(row_id == k, pivot, pivots)
            heads = [held[own][t][k : k + 1, :] * reciprocal for t in range(s + 1, STRIP)]
            pivot_row, pivot_inverse = rows[own][k : k + 1, :], inverse[own][k : k + 1, :]
            for g in range(own, groups):
                base = held[g][s]
                for t in range(s + 1, STRIP):
                    held[g][t] = held[g][t] - base * heads[t - s - 1]
                factor = base * reciprocal
                if g == own:
                    factor = jnp.where(row_id > k, factor, 0.0)
                rows[g] = rows[g] - widen(factor, lanes) * pivot_row
                inverse[g] = inverse[g] - widen(factor, inverse_lanes) * pivot_inverse
            if k == GROUP - 1:
                scale = lax.rsqrt(pivots)
                rows[own] = rows[own] * widen(scale, lanes)
                inverse[own] = inverse[own] * widen(scale, inverse_lanes)
    return rows, inverse


def inverse_factor(gram, inv, beside):
    n = gram.shape[0]
    eye = lax.broadcasted_iota(jnp.int32, (n, n), 0) == lax.broadcasted_iota(jnp.int32, (n, n), 1)
    inv[...] = eye.astype(F32)
    for start in range(0, n, NB):
        done = start + NB
        left = start // 128 * 128
        right = -(-done // 128) * 128
        groups = [pl.ds(start + g, GROUP) for g in range(0, NB, GROUP)]
        beside(start // NB)
        upper, lower = eliminate(
            [gram[g, left:] for g in groups], [inv[g, :right] for g in groups], start - left
        )
        upper, lower = jnp.concatenate(upper, axis=0), jnp.concatenate(lower, axis=0)
        inv[pl.ds(start, NB), :right] = lower
        if done < n:
            keep = done // 128 * 128
            upper_parts = split(upper[:, keep - left :])
            factor = stacked(upper_parts, LEFT)
            rest = pl.ds(done, n - done)
            update = dot(factor, stacked(upper_parts, RIGHT), TN)
            gram[rest, keep:] = gram[rest, keep:] - update[done - keep :]
            update = dot(factor, stacked(split(lower), RIGHT), TN)
            inv[rest, :right] = inv[rest, :right] - update[done - keep :]


def first_kernel(keys_hbm, basis_hbm, out, keys, basis, key_sems, basis_sems):
    width = keys.shape[1] // NX
    copies = []
    for x in range(NX):
        part = pl.ds(x * width, width)
        of_basis = pltpu.make_async_copy(basis_hbm.at[part, :], basis.at[part, :], basis_sems.at[x])
        of_keys = pltpu.make_async_copy(keys_hbm.at[:, part], keys.at[:, part], key_sems.at[x])
        of_basis.start()
        of_keys.start()
        copies.append((of_basis, of_keys))
    projected = 0.0
    for x, (of_basis, of_keys) in enumerate(copies):
        of_basis.wait()
        rounded = basis[pl.ds(x * width, width), :].T.astype(BF16)
        of_keys.wait()
        projected = projected + dot(rounded, keys[:, x * width : (x + 1) * width], NT)
    projected = projected.astype(BF16)
    for x in range(NX):
        out[x] = dot(projected, keys[:, x * width : (x + 1) * width], NN).astype(out.dtype)


def basis_blocks(summed, inv):
    high, mid, _ = split(inv)
    return [dot(high, summed[x], NN) + dot(mid, summed[x], NN) for x in range(NX)]


def factorize(summed, gram, inv, multiply):
    total = 0.0
    for x in range(NX):
        total = total + dot(summed[x], summed[x], NT)
    gram[...] = total
    blocks = gram.shape[0] // NB

    def beside(block):
        if block >= blocks - CHUNKS:
            multiply(block - (blocks - CHUNKS))

    inverse_factor(gram, inv, beside)


def two_part(a):
    high, mid, _ = split(a)
    return high, mid


def three_products(a, b, dims):
    (a_high, a_mid), (b_high, b_mid) = two_part(a), two_part(b)
    return dot(a_high, b_high, dims) + dot(a_high, b_mid, dims) + dot(a_mid, b_high, dims)


def middle_kernel(blocks, keys_hbm, out, gram, inv, mixed, keys, sem):
    copy = pltpu.make_async_copy(keys_hbm, keys, sem)
    copy.start()
    width = blocks.shape[4]
    size = keys.shape[0] // CHUNKS
    parts = [
        [jnp.concatenate([blocks[x, z, p] for z in range(NZ_LOW)], axis=0) for x in range(NX)]
        for p in range(blocks.shape[2])
    ]

    def multiply(chunk):
        if chunk == 0:
            copy.wait()
        at = chunk * size
        total = 0.0
        for part in parts:
            for x in range(NX):
                total = total + dot(part[x], keys[at : at + size, x * width : (x + 1) * width], NT)
        mixed[:, at : at + size] = total

    factorize(parts[0], gram, inv, multiply)
    projected = three_products(inv[...], mixed[...], NN).astype(BF16)
    for x in range(NX):
        out[x] = dot(projected, keys[:, x * width : (x + 1) * width], NN).astype(out.dtype)


def last_kernel(summed, keys_hbm, inv, out, gram, mixed, keys, sem):
    copy = pltpu.make_async_copy(keys_hbm, keys, sem)
    copy.start()
    width = summed.shape[2]
    size = keys.shape[0] // CHUNKS

    def multiply(chunk):
        if chunk == 0:
            copy.wait()
        at = chunk * size
        total = 0.0
        for x in range(NX):
            total = total + dot(keys[at : at + size, x * width : (x + 1) * width], summed[x], NT)
        mixed[at : at + size, :] = total

    factorize(summed, gram, inv, multiply)
    out[...] = three_products(mixed[...], inv[...], NT).astype(BF16)


def basis_kernel(summed, inv, out):
    width = summed.shape[2]
    scale = jnp.sqrt(F32(NX * width))
    for x, block in enumerate(basis_blocks(summed, inv[...])):
        out[pl.ds(x * width, width), :] = (block * scale).T


def call(body, out_shape, operands, in_hbm, scratch, cost=None):
    spec = [pl.BlockSpec(memory_space=pltpu.HBM if h else pltpu.VMEM) for h in in_hbm]
    return pl.pallas_call(
        body,
        out_shape=out_shape,
        in_specs=spec,
        out_specs=jax.tree.map(lambda _: pl.BlockSpec(memory_space=pltpu.VMEM), out_shape),
        scratch_shapes=scratch,
        cost_estimate=cost,
        compiler_params=pltpu.CompilerParams(vmem_limit_bytes=VMEM_BYTES),
    )(*operands)


def add_up(terms):
    terms = [terms[i].astype(F32) for i in range(terms.shape[0])]
    while len(terms) > 1:
        terms = [a + b for a, b in zip(terms[0::2], terms[1::2])]
    return terms[0]


def sum_and_spread(local_term, sums, parts):
    _, rank, width = local_term.shape
    near = NX * NZ_LOW
    part = rank // NZ_LOW
    terms = local_term.reshape(near, part, width)
    terms = lax.all_to_all(terms, POS, 0, 0, axis_index_groups=NEAR, tiled=True)
    own = add_up(terms).astype(sums)
    for pairs in PAIRS:
        both_ways = [
            (x * NZ + p, x * NZ + q) for x in range(NX) for a, b in pairs for p, q in ((a, b), (b, a))
        ]
        other = lax.ppermute(own, POS, both_ways)
        own = (own.astype(F32) + other.astype(F32)).astype(sums)
    total = jnp.stack(split(own.astype(F32))[:parts]) if parts > 1 else own.astype(BF16)[None]
    total = jnp.broadcast_to(total[None], (near, parts, part, width))
    blocks = lax.all_to_all(total, POS, 0, 0, axis_index_groups=NEAR, tiled=True)
    return blocks.reshape(NX, NZ_LOW, parts, part, width)


def local(key_cache, init_basis):
    positions, features = key_cache.shape
    rank = init_basis.shape[1]
    width = features // NX
    shape = jax.ShapeDtypeStruct
    square = pltpu.VMEM((rank, rank), F32)
    keys = pltpu.VMEM((positions, features), BF16)
    sem = pltpu.SemaphoreType.DMA
    blocks = shape((NX, rank, width), BF16)

    scratch = [keys, pltpu.VMEM((features, rank), F32), sem((NX,)), sem((NX,))]
    term = call(first_kernel, blocks, (key_cache, init_basis), (True, True), scratch)
    for sweep in range(ITERS - 1):
        summed = sum_and_spread(term, SUMS, PARTS)
        scratch = [square, square, pltpu.VMEM((rank, positions), F32), keys, sem]
        term = call(middle_kernel, blocks, (summed, key_cache), (False, True), scratch)
    summed = sum_and_spread(term, BF16, 1).reshape(NX, rank, width)
    outs = (shape((rank, rank), F32), shape((positions, rank), BF16))
    scratch = [square, pltpu.VMEM((positions, rank), F32), keys, sem]
    inv, compressed = call(last_kernel, outs, (summed, key_cache), (False, True), scratch)
    latents = lax.all_to_all(
        compressed, ("x", "z_high", "z_low"), split_axis=0, concat_axis=0, tiled=True
    )
    cost = pl.CostEstimate(
        flops=4 * rank * rank * features, bytes_accessed=8 * features * rank, transcendentals=0
    )
    basis = call(basis_kernel, shape((features, rank), F32), (summed, inv), (False, False), [], cost)
    return basis, latents


def solution(mesh):
    grid = Mesh(mesh.devices.reshape(NX, NZ_HIGH, NZ_LOW, -1), AXES)
    return jax.shard_map(
        local,
        mesh=grid,
        in_specs=(P(("grp",) + AXES[:3], None), P("grp", None)),
        out_specs=(P("grp", None), P(("grp",) + AXES[:3], None)),
        check_vma=False,
    )
```

```python
import jax
import jax.numpy as jnp
from jax import lax
from jax.experimental import pallas as pl
from jax.experimental.pallas import tpu as pltpu
from jax.sharding import Mesh
from jax.sharding import PartitionSpec as P

ITERS = 3
NX = 4
NZ_HIGH = 4
NZ_LOW = 2
NB = 32
GROUP = 8
CHUNKS = 4
STRIP = 16
NZ = NZ_HIGH * NZ_LOW
AXES = ("x", "z_high", "z_low", "grp")
POS = AXES[:3]
NEAR = [
    [x * NZ + 2 * high + (low ^ (high % 2)) for low in range(NZ_LOW) for x in range(NX)]
    for high in range(NZ_HIGH)
]
PAIRS = (((0, 3), (2, 5), (4, 7), (6, 1)), ((1, 2), (3, 4), (5, 6), (7, 0)))
VMEM_BYTES = 54_000_000
F32 = jnp.float32
BF16 = jnp.bfloat16

SUMS = F32
PARTS = 2

NN = (((1,), (0,)), ((), ()))
NT = (((1,), (1,)), ((), ()))
TN = (((0,), (0,)), ((), ()))


def dot(a, b, dims):
    return lax.dot_general(a, b, dims, preferred_element_type=F32)


def split(a):
    high = a.astype(BF16)
    rest = a - high.astype(F32)
    mid = rest.astype(BF16)
    low = (rest - mid.astype(F32)).astype(BF16)
    return high, mid, low


def stacked(parts, order):
    return jnp.concatenate([parts[i] for i in order], axis=0)


LEFT = (0, 0, 1, 0, 2, 1)
RIGHT = (0, 1, 0, 2, 0, 1)


def widen(a, lanes):
    return jnp.concatenate([a] * (lanes // 128), axis=1) if lanes > 128 else a


def eliminate(rows, inverse, column):
    row_id = lax.broadcasted_iota(jnp.int32, (GROUP, 128), 0)
    groups = len(rows)
    rows, inverse = list(rows), list(inverse)
    lanes, inverse_lanes = rows[0].shape[1], inverse[0].shape[1]
    for first in range(0, groups, STRIP // GROUP):
        held = {}
        for g in range(first, groups):
            at = column + first * GROUP
            held[g] = [
                jnp.broadcast_to(rows[g][:, at + s : at + s + 1], (GROUP, 128)) for s in range(STRIP)
            ]
        for s in range(STRIP):
            own, k = first + s // GROUP, s % GROUP
            if k == 0:
                pivots = jnp.ones((GROUP, 128), F32)
            pivot = held[own][s][k : k + 1, :]
            reciprocal = 1.0 / pivot
            pivots = jnp.where(row_id == k, pivot, pivots)
            heads = [held[own][t][k : k + 1, :] * reciprocal for t in range(s + 1, STRIP)]
            pivot_row, pivot_inverse = rows[own][k : k + 1, :], inverse[own][k : k + 1, :]
            for g in range(own, groups):
                base = held[g][s]
                for t in range(s + 1, STRIP):
                    held[g][t] = held[g][t] - base * heads[t - s - 1]
                factor = base * reciprocal
                if g == own:
                    factor = jnp.where(row_id > k, factor, 0.0)
                rows[g] = rows[g] - widen(factor, lanes) * pivot_row
                inverse[g] = inverse[g] - widen(factor, inverse_lanes) * pivot_inverse
            if k == GROUP - 1:
                scale = lax.rsqrt(pivots)
                rows[own] = rows[own] * widen(scale, lanes)
                inverse[own] = inverse[own] * widen(scale, inverse_lanes)
    return rows, inverse


def inverse_factor(gram, inv, beside):
    n = gram.shape[0]
    eye = lax.broadcasted_iota(jnp.int32, (n, n), 0) == lax.broadcasted_iota(jnp.int32, (n, n), 1)
    inv[...] = eye.astype(F32)
    for start in range(0, n, NB):
        done = start + NB
        left = start // 128 * 128
        right = -(-done // 128) * 128
        groups = [pl.ds(start + g, GROUP) for g in range(0, NB, GROUP)]
        beside(start // NB)
        upper, lower = eliminate(
            [gram[g, left:] for g in groups], [inv[g, :right] for g in groups], start - left
        )
        upper, lower = jnp.concatenate(upper, axis=0), jnp.concatenate(lower, axis=0)
        inv[pl.ds(start, NB), :right] = lower
        if done < n:
            keep = done // 128 * 128
            upper_parts = split(upper[:, keep - left :])
            factor = stacked(upper_parts, LEFT)
            rest = pl.ds(done, n - done)
            update = dot(factor, stacked(upper_parts, RIGHT), TN)
            gram[rest, keep:] = gram[rest, keep:] - update[done - keep :]
            update = dot(factor, stacked(split(lower), RIGHT), TN)
            inv[rest, :right] = inv[rest, :right] - update[done - keep :]


def first_kernel(keys_hbm, basis_hbm, out, keys, basis, key_sems, basis_sems):
    width = keys.shape[1] // NX
    copies = []
    for x in range(NX):
        part = pl.ds(x * width, width)
        of_basis = pltpu.make_async_copy(basis_hbm.at[part, :], basis.at[part, :], basis_sems.at[x])
        of_keys = pltpu.make_async_copy(keys_hbm.at[:, part], keys.at[:, part], key_sems.at[x])
        of_basis.start()
        of_keys.start()
        copies.append((of_basis, of_keys))
    projected = 0.0
    for x, (of_basis, of_keys) in enumerate(copies):
        of_basis.wait()
        rounded = basis[pl.ds(x * width, width), :].T.astype(BF16)
        of_keys.wait()
        projected = projected + dot(rounded, keys[:, x * width : (x + 1) * width], NT)
    projected = projected.astype(BF16)
    for x in range(NX):
        out[x] = dot(projected, keys[:, x * width : (x + 1) * width], NN).astype(out.dtype)


def basis_blocks(summed, inv):
    high, mid, _ = split(inv)
    return [dot(high, summed[x], NN) + dot(mid, summed[x], NN) for x in range(NX)]


def factorize(summed, gram, inv, multiply):
    total = 0.0
    for x in range(NX):
        total = total + dot(summed[x], summed[x], NT)
    gram[...] = total
    blocks = gram.shape[0] // NB

    def beside(block):
        if block >= blocks - CHUNKS:
            multiply(block - (blocks - CHUNKS))

    inverse_factor(gram, inv, beside)


def two_part(a):
    high, mid, _ = split(a)
    return high, mid


def three_products(a, b, dims):
    (a_high, a_mid), (b_high, b_mid) = two_part(a), two_part(b)
    return dot(a_high, b_high, dims) + dot(a_high, b_mid, dims) + dot(a_mid, b_high, dims)


def middle_kernel(blocks, keys_hbm, out, gram, inv, mixed, keys, sem):
    copy = pltpu.make_async_copy(keys_hbm, keys, sem)
    copy.start()
    width = blocks.shape[4]
    size = keys.shape[0] // CHUNKS
    parts = [
        [jnp.concatenate([blocks[x, z, p] for z in range(NZ_LOW)], axis=0) for x in range(NX)]
        for p in range(blocks.shape[2])
    ]

    def multiply(chunk):
        if chunk == 0:
            copy.wait()
        at = chunk * size
        total = 0.0
        for part in parts:
            for x in range(NX):
                total = total + dot(part[x], keys[at : at + size, x * width : (x + 1) * width], NT)
        mixed[:, at : at + size] = total

    factorize(parts[0], gram, inv, multiply)
    projected = three_products(inv[...], mixed[...], NN).astype(BF16)
    for x in range(NX):
        out[x] = dot(projected, keys[:, x * width : (x + 1) * width], NN).astype(out.dtype)


def last_kernel(summed, keys_hbm, inv, out, gram, mixed, keys, sem):
    copy = pltpu.make_async_copy(keys_hbm, keys, sem)
    copy.start()
    width = summed.shape[2]
    size = keys.shape[0] // CHUNKS

    def multiply(chunk):
        if chunk == 0:
            copy.wait()
        at = chunk * size
        total = 0.0
        for x in range(NX):
            total = total + dot(keys[at : at + size, x * width : (x + 1) * width], summed[x], NT)
        mixed[at : at + size, :] = total

    factorize(summed, gram, inv, multiply)
    out[...] = three_products(mixed[...], inv[...], NT).astype(BF16)


def basis_kernel(summed, inv, out):
    width = summed.shape[2]
    scale = jnp.sqrt(F32(NX * width))
    for x, block in enumerate(basis_blocks(summed, inv[...])):
        out[pl.ds(x * width, width), :] = (block * scale).T


def call(body, out_shape, operands, in_hbm, scratch, cost=None):
    spec = [pl.BlockSpec(memory_space=pltpu.HBM if h else pltpu.VMEM) for h in in_hbm]
    return pl.pallas_call(
        body,
        out_shape=out_shape,
        in_specs=spec,
        out_specs=jax.tree.map(lambda _: pl.BlockSpec(memory_space=pltpu.VMEM), out_shape),
        scratch_shapes=scratch,
        cost_estimate=cost,
        compiler_params=pltpu.CompilerParams(vmem_limit_bytes=VMEM_BYTES),
    )(*operands)


def add_up(terms):
    terms = [terms[i].astype(F32) for i in range(terms.shape[0])]
    while len(terms) > 1:
        terms = [a + b for a, b in zip(terms[0::2], terms[1::2])]
    return terms[0]


def sum_and_spread(local_term, sums, parts):
    _, rank, width = local_term.shape
    near = NX * NZ_LOW
    part = rank // NZ_LOW
    terms = local_term.reshape(near, part, width)
    terms = lax.all_to_all(terms, POS, 0, 0, axis_index_groups=NEAR, tiled=True)
    own = add_up(terms).astype(sums)
    for pairs in PAIRS:
        both_ways = [
            (x * NZ + p, x * NZ + q) for x in range(NX) for a, b in pairs for p, q in ((a, b), (b, a))
        ]
        other = lax.ppermute(own, POS, both_ways)
        own = (own.astype(F32) + other.astype(F32)).astype(sums)
    total = jnp.stack(split(own.astype(F32))[:parts]) if parts > 1 else own.astype(BF16)[None]
    total = jnp.broadcast_to(total[None], (near, parts, part, width))
    blocks = lax.all_to_all(total, POS, 0, 0, axis_index_groups=NEAR, tiled=True)
    return blocks.reshape(NX, NZ_LOW, parts, part, width)


def local(key_cache, init_basis):
    positions, features = key_cache.shape
    rank = init_basis.shape[1]
    width = features // NX
    shape = jax.ShapeDtypeStruct
    square = pltpu.VMEM((rank, rank), F32)
    keys = pltpu.VMEM((positions, features), BF16)
    sem = pltpu.SemaphoreType.DMA
    blocks = [shape((NX, rank, width), SUMS)] * (ITERS - 1) + [shape((NX, rank, width), BF16)]

    scratch = [keys, pltpu.VMEM((features, rank), F32), sem((NX,)), sem((NX,))]
    term = call(first_kernel, blocks[0], (key_cache, init_basis), (True, True), scratch)
    for sweep in range(ITERS - 1):
        summed = sum_and_spread(term, SUMS, PARTS)
        scratch = [square, square, pltpu.VMEM((rank, positions), F32), keys, sem]
        term = call(middle_kernel, blocks[sweep + 1], (summed, key_cache), (False, True), scratch)
    summed = sum_and_spread(term, BF16, 1).reshape(NX, rank, width)
    outs = (shape((rank, rank), F32), shape((positions, rank), BF16))
    scratch = [square, pltpu.VMEM((positions, rank), F32), keys, sem]
    inv, compressed = call(last_kernel, outs, (summed, key_cache), (False, True), scratch)
    latents = lax.all_to_all(
        compressed, ("x", "z_high", "z_low"), split_axis=0, concat_axis=0, tiled=True
    )
    cost = pl.CostEstimate(
        flops=4 * rank * rank * features, bytes_accessed=8 * features * rank, transcendentals=0
    )
    basis = call(basis_kernel, shape((features, rank), F32), (summed, inv), (False, False), [], cost)
    return basis, latents


def solution(mesh):
    grid = Mesh(mesh.devices.reshape(NX, NZ_HIGH, NZ_LOW, -1), AXES)
    return jax.shard_map(
        local,
        mesh=grid,
        in_specs=(P(("grp",) + AXES[:3], None), P("grp", None)),
        out_specs=(P("grp", None), P(("grp",) + AXES[:3], None)),
        check_vma=False,
    )
```
